256 devices in a mesh: leaf: 64 (over z, y, core), rows: 4 (over x).
Axes of the slice: x: 4, y: 4, z: 8, core: 2. Of those that a mesh axis runs over, the one named last changes fastest.
Arguments:
- leaf_rhs: float32 [32, 1024, 512], P(None, 'leaf', 'rows'), may hold values from -6 to 6
- top_rhs: float32 [32, 2048], replicated, may hold values from -6 to 6
- leaf_inverse: float32 [1024, 512, 512], P('leaf', 'rows'), may hold values from -2 to 2, as said below
- leaf_below: float32 [1024, 512, 512], P('leaf', 'rows'), may hold values from -0.015625 to 0.015625
- row_map: int32 [1024, 512], P('leaf', 'rows'), may hold values from 0 to 2047
- top_inverse: float32 [4, 512, 512], P(None, 'rows'), may hold values from -2 to 2, as said below
Outputs:
- leaf_solution: float32 [32, 1024, 512], P(None, 'leaf', 'rows')
- top_solution: float32 [32, 2048], replicated
The draws below stay inside these ranges and needn't reach their ends.
Inputs may be any that keep to these rules, and one draw needn't show every extreme that they name: `leaf_inverse`: lower triangular, diagonal entries positive. `top_inverse`: lower triangular, diagonal entries positive.
All inputs are finite; a program needn't handle non-finite values.
Results may differ from the reference program's by a relative error of at most 0.000068.
Values sent between devices are 32-bit elements; how exact they have to be, the bound alone decides.
A program may use at most 64 MiB of HBM per device.

```python
import jax
import jax.numpy as jnp
from jax import lax

K = 32
W = 512
R = 512
S = 512
NT = 4
NSUP = 1024
TOPCOLS = 2048


def lower_factor(random_noise, diagonal_values, order):
    row_index = lax.broadcasted_iota(jnp.int32, (order, order), 0)
    col_index = lax.broadcasted_iota(jnp.int32, (order, order), 1)
    strict_part = jnp.where(row_index > col_index, random_noise * order ** (-0.5), 0.0)
    return strict_part + jnp.where(row_index == col_index, diagonal_values, 0.0)


def draw_leaf_inverse(key, part):
    key = jax.random.fold_in(key, 11)
    key_noise, key_diag = jax.random.split(key)
    full_shape = (NSUP, W, W)
    random_noise = jax.random.normal(key_noise, full_shape, jnp.float32)
    diagonal_values = jax.random.uniform(key_diag, full_shape, jnp.float32, 0.5, 1.5)
    return jnp.clip(lower_factor(random_noise, diagonal_values, W), -2.0, 2.0)


def draw_top_inverse(key, part):
    key = jax.random.fold_in(key, 23)
    key_noise, key_diag = jax.random.split(key)
    full_shape = (NT, S, S)
    random_noise = jax.random.normal(key_noise, full_shape, jnp.float32)
    diagonal_values = jax.random.uniform(key_diag, full_shape, jnp.float32, 0.5, 1.5)
    return jnp.clip(lower_factor(random_noise, diagonal_values, S), -2.0, 2.0)


def plant(entries, own_key, smallest, high):
    longest = entries.shape.index(max(entries.shape))
    spots = []
    for shift in (0, 1):
        where = [jax.random.randint(jax.random.fold_in(own_key, axis), (), 0, length) for axis, length in enumerate(entries.shape)]
        where[longest] = (where[longest] + shift) % entries.shape[longest]
        spots.append(tuple(where))
    return entries.at[spots[0]].set(smallest).at[spots[1]].set(high)


def block_levels(key, extent, pieces, low, top_value):
    level = 1.0
    for position, shards_of in pieces:
        steps = jax.random.uniform(jax.random.fold_in(jax.random.fold_in(key, 6), position), (shards_of,), jnp.float32, low / len(pieces), top_value / len(pieces))
        level = level * jnp.repeat(jnp.exp(steps), extent[position] // shards_of).reshape((-1,) + (1,) * (len(extent) - 1 - position))
    return level


def noise(rng, shape, width, most, cuts=(), dtype=jnp.bfloat16):
    result = jax.random.normal(rng, shape, jnp.float32) * width
    if len(cuts) > 0:
        result = block_levels(rng, shape, cuts, -0.22, 0.18) * result
    return jnp.clip(result, min=-most, max=most).astype(dtype)


def setup_inputs(seed: int = 0) -> dict:
    splits = jax.random.split(jax.random.key(seed), 7)
    leaf_rhs = noise(splits[0], (K, NSUP, W), 1.0, 6.0, ((1, 64), (2, 4)), jnp.float32)
    top_rhs = noise(splits[1], (K, TOPCOLS), 1.0, 6.0, (), jnp.float32)
    leaf_inverse = draw_leaf_inverse(jax.random.fold_in(splits[6], 71), 0)
    leaf_below = noise(splits[3], (NSUP, R, W), (W * NSUP * R // TOPCOLS) ** -0.5, 0.015625, ((0, 64), (1, 4)), jnp.float32)
    row_map = plant(jax.random.randint(splits[4], (NSUP, R), 0, TOPCOLS), jax.random.fold_in(splits[4], 1), 0, TOPCOLS - 1).astype(jnp.int32)
    top_inverse = draw_top_inverse(jax.random.fold_in(splits[6], 71), 0)
    return dict(leaf_rhs=leaf_rhs, top_rhs=top_rhs, leaf_inverse=leaf_inverse, leaf_below=leaf_below, row_map=row_map, top_inverse=top_inverse)


def reference(leaf_rhs, top_rhs, leaf_inverse, leaf_below, row_map, top_inverse):
    highest = lax.Precision.HIGHEST
    count_rhs = leaf_rhs.shape[0]
    leaf_forward = jnp.einsum("nvw,knw->knv", leaf_inverse, leaf_rhs, precision=highest)
    below_update = jnp.einsum("nrw,knw->knr", leaf_below, leaf_forward, precision=highest)
    gathered_update = jnp.zeros((count_rhs, TOPCOLS), jnp.float32).at[:, row_map.reshape(-1)].add(below_update.reshape(count_rhs, -1))
    top_forward_rhs = (top_rhs - gathered_update).reshape(count_rhs, NT, S)
    top_forward = jnp.einsum("tvs,kts->ktv", top_inverse, top_forward_rhs, precision=highest)
    top_solution = jnp.einsum("tvs,ktv->kts", top_inverse, top_forward, precision=highest).reshape(count_rhs, TOPCOLS)
    picked_rows = top_solution[:, row_map]
    leaf_corrected = leaf_forward - jnp.einsum("nrw,knr->knw", leaf_below, picked_rows, precision=highest)
    leaf_solution = jnp.einsum("nvw,knv->knw", leaf_inverse, leaf_corrected, precision=highest)
    return leaf_solution, top_solution
```

```python
import functools

import jax
import jax.numpy as jnp
from jax import lax
from jax.experimental import pallas as pl
from jax.experimental.pallas import tpu as pltpu
from jax.sharding import PartitionSpec as P

F32 = jnp.float32
BF16 = jnp.bfloat16
NT_DIMS = (((1,), (1,)), ((), ()))
NN_DIMS = (((1,), (0,)), ((), ()))

NX = 4
G = 2
LANES = 128

F_SKEW = (0, 1, 3, 5)
B_SKEW = (0, 2, 4, 6, 8)


def split(v):
    hi = v.astype(BF16)
    lo = (v - hi.astype(F32)).astype(BF16)
    return hi, lo


def mm_nt(x, w):
    m = x.shape[0]
    hi, lo = split(x)
    o = lax.dot_general(jnp.concatenate([hi, lo], 0), w, NT_DIMS, preferred_element_type=F32)
    return (o[:m, :LANES] + o[:m, LANES:]) + (o[m:, :LANES] + o[m:, LANES:])


def mm_nn(hi, lo, w):
    m = hi.shape[0]
    top = jnp.concatenate([hi, hi], 1)
    low = jnp.concatenate([lo, lo], 1)
    o = lax.dot_general(jnp.concatenate([top, low], 0), w, NN_DIMS, preferred_element_type=F32)
    return o[:m] + o[m:]


def kernel(
    dims,
    rhs_ref, trhs_ref, map_ref, inv_hbm, below_hbm, tinv_hbm,
    leaf_out, top_out,
    a_f32, b_f32, t_f32, a_hl, b_hl, t_hl, onehot,
    gb, gy, upd, zbuf0, ztop, cbuf, yacc, ybuf, zbuf, xbuf, xbuf2, rvec, hl_in, sol, s_hl,
    pb, pa, r1b, r1a, r2b, r2a,
    in_sem, ssem, rsem, tssem, trsem,
):
    nz, ny = dims
    nodes, k = gb.shape[1], gb.shape[2]
    chunks = nodes // G
    nt = t_f32.shape[0]
    half = zbuf0.shape[0] // 2
    yrows = half // ny
    prow = yrows // nz
    kp = prow // 4
    mp = hl_in.shape[0] // 2

    leaf = lax.axis_index("leaf")
    x = lax.axis_index("rows")
    core = lax.rem(leaf, 2)
    y = lax.rem(leaf // 2, ny)
    z = leaf // (2 * ny)
    right, left = lax.rem(x + 1, NX), lax.rem(x + NX - 1, NX)
    opp = lax.rem(x + 2, NX)

    def leaf_of(zz, yy, cc):
        return (zz * ny + yy) * 2 + cc

    xpeers = [lax.rem(x + d, NX) for d in range(1, NX)]
    ypeers = [lax.rem(y + d, ny) for d in range(1, ny)]
    zpeers = [lax.rem(z + d, nz) for d in range(1, nz)]
    partner = leaf_of(z, y, 1 - core)

    barrier = pltpu.get_barrier_semaphore()
    peers = [{"rows": p} for p in xpeers]
    peers += [{"leaf": leaf_of(z, p, core)} for p in ypeers]
    peers += [{"leaf": leaf_of(p, y, core)} for p in zpeers]
    peers += [{"leaf": partner}]
    for p in peers:
        pl.semaphore_signal(barrier, inc=1, device_id=p, device_id_type=pl.DeviceIdType.MESH)

    def load(which, c):
        src, dst = ((inv_hbm, a_f32), (below_hbm, b_f32))[which]
        return pltpu.make_async_copy(src.at[pl.ds(c * G, G)], dst.at[pl.ds(c * G, G)], in_sem.at[which, c])

    def load_top():
        return pltpu.make_async_copy(tinv_hbm, t_f32, in_sem.at[2, 0])

    for which in range(2):
        def start_load(c, _, which=which):
            load(which, c).start()
            return 0

        lax.fori_loop(0, chunks, start_load, 0)
    load_top().start()

    def fill_own(n, _):
        gb[x, n] = rhs_ref[pl.ds(n, k, stride=nodes), :]
        return 0

    lax.fori_loop(0, nodes, fill_own, 0)

    def send(phase, kind, c, src, dst):
        to = right if kind in (0, 2) else left
        return pltpu.make_async_remote_copy(
            src_ref=src, dst_ref=dst,
            send_sem=ssem.at[phase, kind, c], recv_sem=rsem.at[phase, kind, c],
            device_id={"rows": to}, device_id_type=pl.DeviceIdType.MESH,
        )

    def gather_direct(phase, buf, c, kind):
        blk = buf.at[x, pl.ds(c * G, G)]
        return send(phase, kind, c, blk, blk)

    def gather_forward(phase, buf, c, kind):
        blk = buf.at[left if kind == 2 else right, pl.ds(c * G + (kind - 2), 1)]
        return send(phase, kind, c, blk, blk)

    pl.semaphore_wait(barrier, len(peers))

    def start_rhs(c, _):
        gather_direct(0, gb, c, 0).start()
        gather_direct(0, gb, c, 1).start()
        return 0

    lax.fori_loop(0, chunks, start_rhs, 0)

    for t in range(nt):
        for q in range(4):
            ztop[pl.ds(t * 4 * k + q, k, stride=4), :] = trhs_ref[:, pl.ds((t * 4 + q) * LANES, LANES)]
    upd[...] = jnp.zeros(upd.shape, F32)
    hl_in[...] = jnp.zeros(hl_in.shape, F32)

    def store_split(dst, n, v):
        hi, lo = split(v)
        dst[n, 0:LANES, :] = hi
        dst[n, LANES : 2 * LANES, :] = lo

    def stage(i, skew, body):
        c = i - skew

        @pl.when((c >= 0) & (c < chunks))
        def _():
            body(c)

    def full_row(buf, n):
        return jnp.concatenate([buf[s, n] for s in range(NX)], 1)

    def f0(c):
        load(0, c).wait()
        for j in range(G):
            store_split(a_hl, c * G + j, a_f32[c * G + j])
        gather_direct(0, gb, c, 0).wait_recv()
        gather_forward(0, gb, c, 2).start()
        gather_direct(0, gb, c, 1).wait_recv()
        gather_forward(0, gb, c, 3).start()

    def f1(c):
        gather_forward(0, gb, c, 2).wait_recv()
        gather_forward(0, gb, c, 3).wait_recv()
        for j in range(G):
            n = c * G + j
            gy[x, n] = mm_nt(full_row(gb, n), a_hl[n])
        gather_direct(1, gy, c, 0).start()
        gather_direct(1, gy, c, 1).start()

    def f2(c):
        load(1, c).wait()
        for j in range(G):
            n = c * G + j
            store_split(b_hl, n, b_f32[n])
            row = map_ref[pl.ds(n, 1), :]

            def build(s, _, row=row, j=j):
                cols = lax.broadcasted_iota(jnp.int32, (256, LANES), 0) + s * 256
                hot = jnp.where(cols == row, 1.0, 0.0).astype(BF16)
                onehot[c, pl.ds(pl.multiple_of(s * 256, 256), 256), j * LANES : (j + 1) * LANES] = hot
                return 0

            lax.fori_loop(0, onehot.shape[1] // 256, build, 0)
        gather_direct(1, gy, c, 0).wait_recv()
        gather_forward(1, gy, c, 2).start()
        gather_direct(1, gy, c, 1).wait_recv()
        gather_forward(1, gy, c, 3).start()

    def f3(c):
        gather_forward(1, gy, c, 2).wait_recv()
        gather_forward(1, gy, c, 3).wait_recv()
        u = [mm_nt(full_row(gy, c * G + j), b_hl[c * G + j]) for j in range(G)]
        hi, lo = split(jnp.concatenate(u, 1))
        lhs = jnp.concatenate([hi, lo], 0)
        width = 512
        for s in range(onehot.shape[1] // width):
            o = lax.dot_general(
                lhs, onehot[c, s * width : (s + 1) * width, :], NT_DIMS, preferred_element_type=F32
            )
            upd[:, s * width : (s + 1) * width] += o[:k] + o[k:]

    def forward(i, _):
        stage(i, F_SKEW[0], f0)
        stage(i, F_SKEW[1], f1)
        stage(i, F_SKEW[2], f2)
        stage(i, F_SKEW[3], f3)
        return 0

    lax.fori_loop(0, chunks + F_SKEW[3], forward, 0)

    for t in range(nt):
        for q in range(4):
            zbuf0[pl.ds(t * 4 * k + q, k, stride=4), :] = upd[:, (t * 4 + q) * LANES : (t * 4 + q + 1) * LANES]

    def tsend(step, slot, src, dst, to):
        return pltpu.make_async_remote_copy(
            src_ref=src, dst_ref=dst, send_sem=tssem.at[step, slot], recv_sem=trsem.at[step, slot],
            device_id=to, device_id_type=pl.DeviceIdType.MESH,
        )

    def rows_at(start, size):
        return pl.ds(pl.multiple_of(start, 8), size)

    hand = tsend(0, 0, zbuf0.at[rows_at((1 - core) * half, half)], cbuf, {"leaf": partner})
    hand.start()
    load_top().wait()
    for t in range(nt):
        store_split(t_hl, t, t_f32[t])
    hand.wait_recv()
    yacc[...] = zbuf0[rows_at(core * half, half), :] + cbuf[...]

    ysends = [
        tsend(1, d, yacc.at[rows_at(p * yrows, yrows)], ybuf.at[d], {"leaf": leaf_of(z, p, core)})
        for d, p in enumerate(ypeers)
    ]
    for s in ysends:
        s.start()
    total = yacc[rows_at(y * yrows, yrows), :]
    for d, s in enumerate(ysends):
        s.wait_recv()
        total = total + ybuf[d]
    yacc2 = ybuf.at[ny - 1]
    yacc2[...] = total
    zsends = [
        tsend(2, d, yacc2.at[rows_at(p * prow, prow)], zbuf.at[d], {"leaf": leaf_of(p, y, core)})
        for d, p in enumerate(zpeers)
    ]
    for s in zsends:
        s.start()
    total = yacc2[rows_at(z * prow, prow), :]
    for d, s in enumerate(zsends):
        s.wait_recv()
        total = total + zbuf[d]

    def all_x(step, buf, value):
        buf[x] = value
        sends = [tsend(step, d, buf.at[x], buf.at[x], {"rows": p}) for d, p in enumerate(xpeers)]
        for s in sends:
            s.start()
        for s in sends:
            s.wait_recv()
        return sends, (buf[0] + buf[1]) + (buf[2] + buf[3])

    xsends, total = all_x(3, xbuf, total)
    first = core * half + y * yrows + z * prow
    rvec[...] = ztop[rows_at(first, prow), :] - total
    t_mine = first // (4 * k)
    r = jnp.concatenate([rvec[pl.ds(q, kp, stride=4), :] for q in range(4)], 1)
    hi, lo = split(r)
    hl_in[0:kp, :] = hi.astype(F32)
    hl_in[mp : mp + kp, :] = lo.astype(F32)
    o = lax.dot_general(hl_in[...].astype(BF16), t_hl[t_mine], NT_DIMS, preferred_element_type=F32)
    f = (o[:mp, :LANES] + o[:mp, LANES:]) + (o[mp:, :LANES] + o[mp:, LANES:])
    hi, lo = split(f)
    fhl = jnp.concatenate([hi.astype(F32), lo.astype(F32)], 0)
    fhl = jnp.concatenate([fhl, fhl], 1).astype(BF16)
    o = lax.dot_general(fhl, t_hl[t_mine], NN_DIMS, preferred_element_type=F32)
    s_part = o[:mp] + o[mp:]
    for q in range(4):
        rvec[pl.ds(q, kp, stride=4), :] = s_part[0:kp, q * LANES : (q + 1) * LANES]
    xsends2, total = all_x(4, xbuf2, rvec[...])
    sol[rows_at(first, prow), :] = total

    def spread(step, start, size, targets):
        blk = sol.at[rows_at(start, size)]
        sends = [tsend(step, d, blk, blk, to) for d, to in enumerate(targets)]
        for s in sends:
            s.start()
        for s in sends:
            s.wait_recv()
        return sends

    g1 = spread(5, first, prow, [{"leaf": leaf_of(p, y, core)} for p in zpeers])
    g2 = spread(6, core * half + y * yrows, yrows, [{"leaf": leaf_of(z, p, core)} for p in ypeers])
    g3 = spread(7, core * half, half, [{"leaf": partner}])

    for t in range(nt):
        for q in range(4):
            v = sol[pl.ds(t * 4 * k + q, k, stride=4), :]
            at = (t * 4 + q) * LANES
            top_out[:, at : at + LANES] = v
            hi, lo = split(v)
            s_hl[0:k, at : at + LANES] = hi
            s_hl[k : 2 * k, at : at + LANES] = lo

    def toward_opp(phase, buf, r1, c, kind):
        n = c * G + kind
        return send(phase, kind, c, buf.at[opp, pl.ds(n, 1)], r1.at[pl.ds(n, 1)])

    def toward_next(phase, buf, r2, c, kind):
        ns = pl.ds(c * G, G)
        return send(phase, kind, c, buf.at[right if kind == 2 else left, ns], r2.at[kind - 2, ns])

    def put(buf, n, v):
        for s in range(NX):
            buf[s, n] = v[:, s * LANES : (s + 1) * LANES]

    def start_opp(phase, buf, r1, c):
        toward_opp(phase, buf, r1, c, 0).start()
        toward_opp(phase, buf, r1, c, 1).start()

    def add_and_pass(phase, buf, r1, r2, c):
        n = c * G
        toward_opp(phase, buf, r1, c, 0).wait_recv()
        buf[right, n] += r1[n]
        toward_next(phase, buf, r2, c, 2).start()
        toward_opp(phase, buf, r1, c, 1).wait_recv()
        buf[left, n + 1] += r1[n + 1]
        toward_next(phase, buf, r2, c, 3).start()

    def collect(phase, buf, r2, c):
        toward_next(phase, buf, r2, c, 2).wait_recv()
        toward_next(phase, buf, r2, c, 3).wait_recv()
        ns = pl.ds(c * G, G)
        return buf[x, ns] + (r2[0, ns] + r2[1, ns])

    def b0(c):
        picked = lax.dot_general(s_hl[...], onehot[c], NN_DIMS, preferred_element_type=F32).astype(BF16)
        for j in range(G):
            at = slice(j * LANES, (j + 1) * LANES)
            put(pb, c * G + j, mm_nn(picked[:k, at], picked[k:, at], b_hl[c * G + j]))
        start_opp(2, pb, r1b, c)

    def b1(c):
        add_and_pass(2, pb, r1b, r2b, c)

    def b2(c):
        back = collect(2, pb, r2b, c)
        for j in range(G):
            n = c * G + j
            hi, lo = split(gy[x, n] - back[j])
            put(pa, n, mm_nn(hi, lo, a_hl[n]))
        start_opp(3, pa, r1a, c)

    def b3(c):
        add_and_pass(3, pa, r1a, r2a, c)

    def b4(c):
        done = collect(3, pa, r2a, c)
        for j in range(G):
            leaf_out[pl.ds(c * G + j, k, stride=nodes), :] = done[j]

    def backward(i, _):
        for skew, body in zip(B_SKEW, (b0, b1, b2, b3, b4)):
            stage(i, skew, body)
        return 0

    lax.fori_loop(0, chunks + B_SKEW[4], backward, 0)

    def drain(c, _):
        for phase, buf in ((0, gb), (1, gy)):
            for kind in (0, 1):
                gather_direct(phase, buf, c, kind).wait_send()
                gather_forward(phase, buf, c, kind + 2).wait_send()
        for phase, buf, r1, r2 in ((2, pb, r1b, r2b), (3, pa, r1a, r2a)):
            for kind in (0, 1):
                toward_opp(phase, buf, r1, c, kind).wait_send()
                toward_next(phase, buf, r2, c, kind + 2).wait_send()
        return 0

    lax.fori_loop(0, chunks, drain, 0)
    for s in [hand] + ysends + zsends + xsends + xsends2 + g1 + g2 + g3:
        s.wait_send()


def make(nz, ny):
    def on_device(leaf_rhs, top_rhs, leaf_inverse, leaf_below, row_map, top_inverse):
        k, nodes, width = leaf_rhs.shape
        nt, _, s = top_inverse.shape
        full = leaf_inverse.shape[2]
        cols = top_rhs.shape[1]
        chunks = nodes // G
        rows = cols * k // LANES
        half = rows // 2
        yrows = half // ny
        prow = yrows // nz
        mp = max(8, prow // 4)
        vmem = pl.BlockSpec(memory_space=pltpu.VMEM)
        hbm = pl.BlockSpec(memory_space=pl.ANY)
        blocks = (NX, nodes, k, LANES)
        scratch = [
            pltpu.VMEM(leaf_inverse.shape, F32),
            pltpu.VMEM(leaf_below.shape, F32),
            pltpu.VMEM(top_inverse.shape, F32),
            pltpu.VMEM((nodes, 2 * LANES, full), BF16),
            pltpu.VMEM((nodes, 2 * LANES, full), BF16),
            pltpu.VMEM((nt, 2 * LANES, s), BF16),
            pltpu.VMEM((chunks, cols, G * LANES), BF16),
            pltpu.VMEM(blocks, F32),
            pltpu.VMEM(blocks, F32),
            pltpu.VMEM((k, cols), F32),
            pltpu.VMEM((rows, LANES), F32),
            pltpu.VMEM((rows, LANES), F32),
            pltpu.VMEM((half, LANES), F32),
            pltpu.VMEM((half, LANES), F32),
            pltpu.VMEM((ny, yrows, LANES), F32),
            pltpu.VMEM((nz, prow, LANES), F32),
            pltpu.VMEM((NX, prow, LANES), F32),
            pltpu.VMEM((NX, prow, LANES), F32),
            pltpu.VMEM((prow, LANES), F32),
            pltpu.VMEM((2 * mp, s), F32),
            pltpu.VMEM((rows, LANES), F32),
            pltpu.VMEM((2 * k, cols), BF16),
            pltpu.VMEM(blocks, F32),
            pltpu.VMEM(blocks, F32),
            pltpu.VMEM(blocks[1:], F32),
            pltpu.VMEM(blocks[1:], F32),
            pltpu.VMEM((2,) + blocks[1:], F32),
            pltpu.VMEM((2,) + blocks[1:], F32),
            pltpu.SemaphoreType.DMA((3, chunks)),
            pltpu.SemaphoreType.DMA((4, 4, chunks)),
            pltpu.SemaphoreType.DMA((4, 4, chunks)),
            pltpu.SemaphoreType.DMA((8, 8)),
            pltpu.SemaphoreType.DMA((8, 8)),
        ]
        macs = nodes * width * full * k
        leaf_solution, top_solution = pl.pallas_call(
            functools.partial(kernel, (nz, ny)),
            out_shape=(
                jax.ShapeDtypeStruct((k * nodes, width), F32),
                jax.ShapeDtypeStruct((k, cols), F32),
            ),
            in_specs=[vmem, vmem, vmem, hbm, hbm, hbm],
            out_specs=(vmem, vmem),
            scratch_shapes=scratch,
            compiler_params=pltpu.CompilerParams(
                collective_id=0, has_side_effects=True, vmem_limit_bytes=52 * 2**20
            ),
            cost_estimate=pl.CostEstimate(flops=24 * macs, bytes_accessed=10 * 2**20, transcendentals=0),
        )(
            leaf_rhs.reshape(k * nodes, width),
            top_rhs,
            row_map,
            leaf_inverse,
            leaf_below,
            top_inverse,
        )
        return leaf_solution.reshape(k, nodes, width), top_solution

    return on_device


def solution(mesh, nz=8, ny=4):
    placed = (
        P(None, "leaf", "rows"),
        P(),
        P("leaf", "rows", None),
        P("leaf", "rows", None),
        P("leaf", "rows"),
        P(None, "rows", None),
    )
    return jax.shard_map(
        make(nz, ny),
        mesh=mesh,
        in_specs=placed,
        out_specs=(P(None, "leaf", "rows"), P()),
        check_vma=False,
    )
```

```python
import functools

import jax
import jax.numpy as jnp
from jax import lax
from jax.experimental import pallas as pl
from jax.experimental.pallas import tpu as pltpu
from jax.sharding import PartitionSpec as P

F32 = jnp.float32
BF16 = jnp.bfloat16
NT_DIMS = (((1,), (1,)), ((), ()))
NN_DIMS = (((1,), (0,)), ((), ()))

NX = 4
G = 4
LANES = 128
H = 2

F_AT = (0, 3, 6, 9)
F_GAP = 3
TOP_AT = ((1, 4, 8, 9, 10, 11, 12), (8, 9, 10, 11, 12, 14, 16))
TAKE_AT = (17, 13)
B_FIRST = 13
B_AT = (0, 3, 6, 9, 12)
B_GAP = 0
STRAIGHT = ((0, 0), (6, 8), (0, 0), (6, 8))
PREP = 4


def split(v):
    hi = v.astype(BF16)
    lo = (v - hi.astype(F32)).astype(BF16)
    return hi, lo


def mm_row(x, w):
    m = x.shape[0]
    hi, lo = split(x)
    o = lax.dot_general(jnp.concatenate([hi, lo], 0), w, NN_DIMS, preferred_element_type=F32)
    return (o[:m, :LANES] + o[:m, LANES:]) + (o[m:, :LANES] + o[m:, LANES:])


def mm_nn(hi, lo, w):
    m = hi.shape[0]
    top = jnp.concatenate([hi, hi], 1)
    low = jnp.concatenate([lo, lo], 1)
    o = lax.dot_general(jnp.concatenate([top, low], 0), w, NN_DIMS, preferred_element_type=F32)
    return o[:m] + o[m:]


def kernel(
    dims,
    rhs_hbm, trhs_hbm, map_hbm, inv_hbm, below_hbm, tinv_hbm,
    leaf_out, top_out,
    rhs_ref, trhs_ref, map_ref, a_f32, b_f32, t_f32, a_hl, b_hl, t_hl, a_t, b_t, hot_in, hot_out,
    gb, gy, upd, urow, ztop, cbuf, yacc, ybuf, zbuf, xbuf, xbuf2, rvec, hl_in, sol, s_hl,
    pb, pa, r1b, r1a, r2b, r2a,
    in_sem, ssem, rsem, tssem, trsem,
):
    nz, ny = dims
    nodes, k = gb.shape[2], gb.shape[3]
    chunks = nodes // G
    units = H * chunks
    nt = t_f32.shape[0]
    cols = upd.shape[2]
    yrows = urow.shape[1] // ny
    prow = yrows // nz
    kp = prow // 4
    mp = hl_in.shape[0] // 2

    leaf = lax.axis_index("leaf")
    x = lax.axis_index("rows")
    core = lax.rem(leaf, 2)
    y = lax.rem(leaf // 2, ny)
    z = leaf // (2 * ny)
    right, left = lax.rem(x + 1, NX), lax.rem(x + NX - 1, NX)
    opp = lax.rem(x + 2, NX)

    def leaf_of(zz, yy, cc):
        return (zz * ny + yy) * 2 + cc

    xpeers = [lax.rem(x + d, NX) for d in range(1, NX)]
    ypeers = [lax.rem(y + d, ny) for d in range(1, ny)]
    zpeers = [lax.rem(z + d, nz) for d in range(1, nz)]
    partner = leaf_of(z, y, 1 - core)

    barrier = pltpu.get_barrier_semaphore()
    peers = [{"rows": p} for p in xpeers]
    peers += [{"leaf": leaf_of(z, p, core)} for p in ypeers]
    peers += [{"leaf": leaf_of(p, y, core)} for p in zpeers]
    peers += [{"leaf": partner}]
    for p in peers:
        pl.semaphore_signal(barrier, inc=1, device_id=p, device_id_type=pl.DeviceIdType.MESH)

    def load(which, c):
        src, dst = ((inv_hbm, a_f32), (below_hbm, b_f32))[which]
        return pltpu.make_async_copy(src.at[pl.ds(c * G, G)], dst.at[pl.ds(c * G, G)], in_sem.at[which, c])

    whole = [
        pltpu.make_async_copy(src, dst, in_sem.at[2, i])
        for i, (src, dst) in enumerate(
            ((rhs_hbm, rhs_ref), (map_hbm, map_ref), (tinv_hbm, t_f32), (trhs_hbm, trhs_ref))
        )
    ]
    whole[0].start()
    whole[1].start()
    for which in range(2):
        def start_load(c, _, which=which):
            load(which, c).start()
            return 0

        lax.fori_loop(0, chunks, start_load, 0)
    whole[2].start()
    whole[3].start()
    whole[0].wait()

    def fill_own(n, _):
        for h in range(H):
            gb[x, h, n] = rhs_ref[pl.ds(h * k * nodes + n, k, stride=nodes), :]
        return 0

    lax.fori_loop(0, nodes, fill_own, 0)

    def store_split(dst, n, v):
        hi, lo = split(v)
        dst[n, 0:LANES, :] = hi
        dst[n, LANES : 2 * LANES, :] = lo

    def store_both(dst, dst_t, n, v):
        hi, lo = split(v)
        dst[n, 0:LANES, :] = hi
        dst[n, LANES : 2 * LANES, :] = lo
        dst_t[n, :, 0:LANES] = hi.T
        dst_t[n, :, LANES : 2 * LANES] = lo.T

    def prepare(c, _):
        load(0, c).wait()
        for j in range(G):
            store_both(a_hl, a_t, c * G + j, a_f32[c * G + j])
        return 0

    def prepare_below(c, _):
        load(1, c).wait()
        for j in range(G):
            store_both(b_hl, b_t, c * G + j, b_f32[c * G + j])
        for j in range(G):
            own = jnp.broadcast_to(map_ref[pl.ds(c * G + j, 1), :], (LANES, LANES)).T
            at = lax.broadcasted_iota(jnp.int32, (LANES, LANES), 1)
            for q in range(cols // LANES):
                hot = jnp.where(own == at + q * LANES, 1.0, 0.0).astype(BF16)
                hot_in[c, j * LANES : (j + 1) * LANES, q * LANES : (q + 1) * LANES] = hot
        return 0

    def prepare_out(u):
        for j in range(G):
            row = map_ref[pl.ds(u * G + j, 1), :]

            def build(s, _, row=row, j=j):
                at = lax.broadcasted_iota(jnp.int32, (256, LANES), 0) + s * 256
                hot = jnp.where(at == row, 1.0, 0.0).astype(BF16)
                hot_out[u, pl.ds(pl.multiple_of(s * 256, 256), 256), j * LANES : (j + 1) * LANES] = hot
                return 0

            lax.fori_loop(0, cols // 256, build, 0)

    whole[1].wait()
    lax.fori_loop(0, PREP, prepare, 0)

    def send(phase, kind, u, src, dst):
        to = opp if kind == 4 else right if kind in (0, 2) else left
        return pltpu.make_async_remote_copy(
            src_ref=src, dst_ref=dst,
            send_sem=ssem.at[phase, kind, u], recv_sem=rsem.at[phase, kind, u],
            device_id={"rows": to}, device_id_type=pl.DeviceIdType.MESH,
        )

    def place(u):
        return lax.div(u, chunks), lax.rem(u, chunks)

    def straight(phase, u):
        low, high = STRAIGHT[phase]
        return (u >= low) & (u < high)

    def gather_direct(phase, u, kind):
        h, c = place(u)
        blk = (gb, gy)[phase].at[x, h, pl.ds(c * G, G)]
        return send(phase, kind, u, blk, blk)

    def gather_forward(phase, u, kind):
        h, c = place(u)
        blk = (gb, gy)[phase].at[left if kind == 2 else right, h, pl.ds(c * G + (kind - 2) * (G // 2), G // 2)]
        return send(phase, kind, u, blk, blk)

    def gather_start(phase, u):
        gather_direct(phase, u, 0).start()
        gather_direct(phase, u, 1).start()

        @pl.when(straight(phase, u))
        def _():
            gather_direct(phase, u, 4).start()

    def gather_pass(phase, u):
        for kind in (0, 1):
            gather_direct(phase, u, kind).wait_recv()

            @pl.when(jnp.logical_not(straight(phase, u)))
            def _(kind=kind):
                gather_forward(phase, u, kind + 2).start()

    def gather_end(phase, u, finish):
        @pl.when(straight(phase, u))
        def _():
            finish(gather_direct(phase, u, 4))

        @pl.when(jnp.logical_not(straight(phase, u)))
        def _():
            finish(gather_forward(phase, u, 2))
            finish(gather_forward(phase, u, 3))

    def arrive(copy):
        copy.wait_recv()

    def leave(copy):
        copy.wait_send()

    pl.semaphore_wait(barrier, len(peers))

    def start_rhs(u, _):
        gather_start(0, u)
        return 0

    lax.fori_loop(0, chunks, start_rhs, 0)

    lax.fori_loop(PREP, chunks, prepare, 0)
    lax.fori_loop(0, chunks, prepare_below, 0)
    whole[2].wait()
    for t in range(nt):
        store_split(t_hl, t, t_f32[t])
    whole[3].wait()
    for t in range(nt):
        for q in range(4):
            at = (t * 4 + q) * LANES
            ztop[pl.ds(t * 4 * k + q, k, stride=4), :] = trhs_ref[
                pl.ds(pl.multiple_of(core * k, 8), k), at : at + LANES
            ]
    upd[...] = jnp.zeros(upd.shape, F32)
    hl_in[...] = jnp.zeros(hl_in.shape, F32)

    def full_row(buf, h, n):
        return jnp.concatenate([buf[s, h, n] for s in range(NX)], 1)

    def tsend(step, slot, src, dst, to):
        return pltpu.make_async_remote_copy(
            src_ref=src, dst_ref=dst, send_sem=tssem.at[step, slot], recv_sem=trsem.at[step, slot],
            device_id=to, device_id_type=pl.DeviceIdType.MESH,
        )

    def rows_at(start, size):
        return pl.ds(pl.multiple_of(start, 8), size)

    def f0(u):
        gather_pass(0, u)

    def f1(u):
        h, c = place(u)
        gather_end(0, u, arrive)
        for j in range(G):
            n = c * G + j
            gy[x, h, n] = mm_row(full_row(gb, h, n), a_t[n])
        gather_start(1, u)

        @pl.when(u + chunks < units)
        def _():
            gather_start(0, u + chunks)

    def f2(u):
        gather_pass(1, u)

    hand = tsend(0, 0, urow.at[1 - core], cbuf, {"leaf": partner})

    def f3(u):
        h, c = place(u)
        gather_end(1, u, arrive)
        v = [mm_row(full_row(gy, h, c * G + j), b_t[c * G + j]) for j in range(G)]
        hi, lo = split(jnp.concatenate(v, 1))
        lhs = jnp.concatenate([hi, lo], 0)
        width = 512
        for s in range(cols // width):
            o = lax.dot_general(
                lhs, hot_in[c, :, s * width : (s + 1) * width], NN_DIMS, preferred_element_type=F32
            )
            upd[h, :, s * width : (s + 1) * width] += o[:k] + o[k:]

        @pl.when(c == chunks - 1)
        def _():
            for t in range(nt):
                for q in range(4):
                    at = (t * 4 + q) * LANES
                    urow[h, pl.ds(t * 4 * k + q, k, stride=4), :] = upd[h, :, at : at + LANES]

            @pl.when(core != h)
            def _():
                hand.start()

    first = y * yrows + z * prow
    t_mine = first // (4 * k)
    ysends = [
        tsend(1, d, yacc.at[rows_at(p * yrows, yrows)], ybuf.at[d], {"leaf": leaf_of(z, p, core)})
        for d, p in enumerate(ypeers)
    ]
    ysum = ybuf.at[ny - 1]
    zsends = [
        tsend(2, d, ysum.at[rows_at(p * prow, prow)], zbuf.at[d], {"leaf": leaf_of(p, y, core)})
        for d, p in enumerate(zpeers)
    ]
    xsends = [tsend(3, d, xbuf.at[x], xbuf.at[x], {"rows": p}) for d, p in enumerate(xpeers)]
    xsends2 = [tsend(4, d, xbuf2.at[x], xbuf2.at[x], {"rows": p}) for d, p in enumerate(xpeers)]
    sol_z = sol.at[core, rows_at(first, prow)]
    sol_y = sol.at[core, rows_at(y * yrows, yrows)]
    zback = [tsend(5, d, sol_z, sol_z, {"leaf": leaf_of(p, y, core)}) for d, p in enumerate(zpeers)]
    yback = [tsend(6, d, sol_y, sol_y, {"leaf": leaf_of(z, p, core)}) for d, p in enumerate(ypeers)]
    give = tsend(7, 0, sol.at[core], sol.at[core], {"leaf": partner})

    def begin(sends):
        for s in sends:
            s.start()

    def t0():
        hand.wait_recv()
        yacc[...] = urow[core] + cbuf[...]
        begin(ysends)

    def t1():
        total = yacc[rows_at(y * yrows, yrows), :]
        for d, s in enumerate(ysends):
            s.wait_recv()
            total = total + ybuf[d]
        ysum[...] = total
        begin(zsends)

    def t2():
        total = ysum[rows_at(z * prow, prow), :]
        for d, s in enumerate(zsends):
            s.wait_recv()
            total = total + zbuf[d]
        xbuf[x] = total
        begin(xsends)

    def t3():
        for s in xsends:
            s.wait_recv()
        rvec[...] = ztop[rows_at(first, prow), :] - ((xbuf[0] + xbuf[1]) + (xbuf[2] + xbuf[3]))
        r = jnp.concatenate([rvec[pl.ds(q, kp, stride=4), :] for q in range(4)], 1)
        hi, lo = split(r)
        hl_in[0:kp, :] = hi.astype(F32)
        hl_in[mp : mp + kp, :] = lo.astype(F32)
        o = lax.dot_general(hl_in[...].astype(BF16), t_hl[t_mine], NT_DIMS, preferred_element_type=F32)
        f = (o[:mp, :LANES] + o[:mp, LANES:]) + (o[mp:, :LANES] + o[mp:, LANES:])
        hi, lo = split(f)
        fhl = jnp.concatenate([hi.astype(F32), lo.astype(F32)], 0)
        fhl = jnp.concatenate([fhl, fhl], 1).astype(BF16)
        o = lax.dot_general(fhl, t_hl[t_mine], NN_DIMS, preferred_element_type=F32)
        s_part = o[:mp] + o[mp:]
        for q in range(4):
            rvec[pl.ds(q, kp, stride=4), :] = s_part[0:kp, q * LANES : (q + 1) * LANES]
        xbuf2[x] = rvec[...]
        begin(xsends2)

    def t4():
        for s in xsends2:
            s.wait_recv()
        sol[core, rows_at(first, prow), :] = (xbuf2[0] + xbuf2[1]) + (xbuf2[2] + xbuf2[3])
        begin(zback)

    def t5():
        for s in zback:
            s.wait_recv()
        begin(yback)

    def t6():
        for s in yback:
            s.wait_recv()
        give.start()
        unpack(core)

    def take():
        tsend(7, 0, sol.at[1 - core], sol.at[1 - core], {"leaf": partner}).wait_recv()
        unpack(1 - core)

    def unpack(h):
        for t in range(nt):
            for q in range(4):
                v = sol[h, pl.ds(t * 4 * k + q, k, stride=4), :]
                at = (t * 4 + q) * LANES
                top_out[pl.ds(pl.multiple_of(h * k, 8), k), at : at + LANES] = v
                hi, lo = split(v)
                s_hl[h, 0:k, at : at + LANES] = hi
                s_hl[h, k : 2 * k, at : at + LANES] = lo

    def toward_opp(phase, u, kind):
        h, c = place(u)
        ns = pl.ds(c * G + kind * (G // 2), G // 2)
        buf, r1 = ((pb, r1b), (pa, r1a))[phase - 2]
        return send(phase, kind, u, buf.at[opp, h, ns], r1.at[h, ns])

    def toward_next(phase, u, kind):
        h, c = place(u)
        ns = pl.ds(c * G, G)
        buf, r2 = ((pb, r2b), (pa, r2a))[phase - 2]
        return send(phase, kind, u, buf.at[(right, left, opp)[kind - 2], h, ns], r2.at[kind - 2, h, ns])

    def put(buf, h, n, v):
        for s in range(NX):
            buf[s, h, n] = v[:, s * LANES : (s + 1) * LANES]

    def reduce_start(phase, u):
        @pl.when(straight(phase, u))
        def _():
            for kind in (2, 3, 4):
                toward_next(phase, u, kind).start()

        @pl.when(jnp.logical_not(straight(phase, u)))
        def _():
            toward_opp(phase, u, 0).start()
            toward_opp(phase, u, 1).start()

    def reduce_pass(phase, u):
        @pl.when(jnp.logical_not(straight(phase, u)))
        def _():
            h, c = place(u)
            buf, r1 = ((pb, r1b), (pa, r1a))[phase - 2]
            for kind, to in ((0, right), (1, left)):
                ns = pl.ds(c * G + kind * (G // 2), G // 2)
                toward_opp(phase, u, kind).wait_recv()
                buf[to, h, ns] += r1[h, ns]
                toward_next(phase, u, kind + 2).start()

    def reduce_end(phase, u):
        h, c = place(u)
        buf, r2 = ((pb, r2b), (pa, r2a))[phase - 2]
        ns = pl.ds(c * G, G)

        @pl.when(straight(phase, u))
        def _():
            toward_next(phase, u, 4).wait_recv()
            buf[x, h, ns] += r2[2, h, ns]

        toward_next(phase, u, 2).wait_recv()
        toward_next(phase, u, 3).wait_recv()
        return buf[x, h, ns] + (r2[0, h, ns] + r2[1, h, ns])

    def b0(u):
        h, c = place(u)
        picked = lax.dot_general(s_hl[h], hot_out[c], NN_DIMS, preferred_element_type=F32).astype(BF16)
        for j in range(G):
            at = slice(j * LANES, (j + 1) * LANES)
            put(pb, h, c * G + j, mm_nn(picked[:k, at], picked[k:, at], b_hl[c * G + j]))
        reduce_start(2, u)

    def b1(u):
        reduce_pass(2, u)

    def b2(u):
        h, c = place(u)
        back = reduce_end(2, u)
        for j in range(G):
            n = c * G + j
            hi, lo = split(gy[x, h, n] - back[j])
            put(pa, h, n, mm_nn(hi, lo, a_hl[n]))
        reduce_start(3, u)

    def b3(u):
        reduce_pass(3, u)

    def b4(u):
        h, c = place(u)
        done = reduce_end(3, u)
        for j in range(G):
            leaf_out[pl.ds(h * k * nodes + c * G + j, k, stride=nodes), :] = done[j]

    def leave_forward(u):
        for phase in (0, 1):
            gather_direct(phase, u, 0).wait_send()
            gather_direct(phase, u, 1).wait_send()
            gather_end(phase, u, leave)

    base = F_AT[3] + chunks - 1
    b_base = base + B_FIRST

    def step(i, _):
        def unit_at(at, gap, body):
            v = i - at
            second = v >= chunks + gap

            @pl.when(((v >= 0) & (v < chunks)) | (second & (v < units + gap)))
            def _():
                body(jnp.where(second, v - gap, v))

        for j, body in enumerate((t0, t1, t2, t3, t4, t5, t6)):
            pl.when(i == base + jnp.where(core == 0, TOP_AT[0][j], TOP_AT[1][j]))(body)
        pl.when(i == base + jnp.where(core == 0, TAKE_AT[0], TAKE_AT[1]))(take)
        unit_at(F_AT[0], F_GAP, f0)
        unit_at(F_AT[2], F_GAP, f2)
        unit_at(F_AT[1], F_GAP, f1)
        unit_at(F_AT[3], F_GAP, f3)
        unit_at(b_base + B_AT[1], B_GAP, b1)
        unit_at(b_base + B_AT[3], B_GAP, b3)
        unit_at(b_base + B_AT[4], B_GAP, b4)
        unit_at(b_base + B_AT[2], B_GAP, b2)
        unit_at(b_base + B_AT[0], B_GAP, b0)
        unit_at(base + TOP_AT[0][2], 0, leave_forward)
        pl.when((i > base) & (i <= base + chunks))(lambda: prepare_out(i - base - 1))
        return 0

    lax.fori_loop(0, b_base + B_AT[4] + units + B_GAP, step, 0)

    def drain(u, _):
        for phase in (2, 3):
            toward_next(phase, u, 2).wait_send()
            toward_next(phase, u, 3).wait_send()

            @pl.when(straight(phase, u))
            def _(phase=phase):
                toward_next(phase, u, 4).wait_send()

            @pl.when(jnp.logical_not(straight(phase, u)))
            def _(phase=phase):
                toward_opp(phase, u, 0).wait_send()
                toward_opp(phase, u, 1).wait_send()

        return 0

    lax.fori_loop(0, units, drain, 0)
    for s in [hand, give] + ysends + zsends + xsends + xsends2 + zback + yback:
        s.wait_send()


def make(nz, ny):
    def on_device(leaf_rhs, top_rhs, leaf_inverse, leaf_below, row_map, top_inverse):
        k, nodes, width = leaf_rhs.shape
        nt, _, s = top_inverse.shape
        full = leaf_inverse.shape[2]
        cols = top_rhs.shape[1]
        chunks = nodes // G
        rows = cols * k // LANES
        half = rows // H
        kh = k // H
        units = H * chunks
        yrows = half // ny
        prow = yrows // nz
        mp = max(8, prow // 4)
        vmem = pl.BlockSpec(memory_space=pltpu.VMEM)
        hbm = pl.BlockSpec(memory_space=pltpu.HBM)
        blocks = (NX, H, nodes, kh, LANES)
        scratch = [
            pltpu.VMEM((k * nodes, width), F32),
            pltpu.VMEM((k, cols), F32),
            pltpu.VMEM((nodes, width), jnp.int32),
            pltpu.VMEM(leaf_inverse.shape, F32),
            pltpu.VMEM(leaf_below.shape, F32),
            pltpu.VMEM(top_inverse.shape, F32),
            pltpu.VMEM((nodes, 2 * LANES, full), BF16),
            pltpu.VMEM((nodes, 2 * LANES, full), BF16),
            pltpu.VMEM((nt, 2 * LANES, s), BF16),
            pltpu.VMEM((nodes, full, 2 * LANES), BF16),
            pltpu.VMEM((nodes, full, 2 * LANES), BF16),
            pltpu.VMEM((chunks, G * LANES, cols), BF16),
            pltpu.VMEM((chunks, cols, G * LANES), BF16),
            pltpu.VMEM(blocks, F32),
            pltpu.VMEM(blocks, F32),
            pltpu.VMEM((H, kh, cols), F32),
            pltpu.VMEM((H, half, LANES), F32),
            pltpu.VMEM((half, LANES), F32),
            pltpu.VMEM((half, LANES), F32),
            pltpu.VMEM((half, LANES), F32),
            pltpu.VMEM((ny, yrows, LANES), F32),
            pltpu.VMEM((nz, prow, LANES), F32),
            pltpu.VMEM((NX, prow, LANES), F32),
            pltpu.VMEM((NX, prow, LANES), F32),
            pltpu.VMEM((prow, LANES), F32),
            pltpu.VMEM((2 * mp, s), F32),
            pltpu.VMEM((H, half, LANES), F32),
            pltpu.VMEM((H, 2 * kh, cols), BF16),
            pltpu.VMEM(blocks, F32),
            pltpu.VMEM(blocks, F32),
            pltpu.VMEM(blocks[1:], F32),
            pltpu.VMEM(blocks[1:], F32),
            pltpu.VMEM((3,) + blocks[1:], F32),
            pltpu.VMEM((3,) + blocks[1:], F32),
            pltpu.SemaphoreType.DMA((3, max(chunks, 4))),
            pltpu.SemaphoreType.DMA((4, 5, units)),
            pltpu.SemaphoreType.DMA((4, 5, units)),
            pltpu.SemaphoreType.DMA((8, 8)),
            pltpu.SemaphoreType.DMA((8, 8)),
        ]
        macs = nodes * width * full * k
        leaf_solution, top_solution = pl.pallas_call(
            functools.partial(kernel, (nz, ny)),
            out_shape=(
                jax.ShapeDtypeStruct((k * nodes, width), F32),
                jax.ShapeDtypeStruct((k, cols), F32),
            ),
            in_specs=[hbm] * 6,
            out_specs=(vmem, vmem),
            scratch_shapes=scratch,
            compiler_params=pltpu.CompilerParams(
                collective_id=0, has_side_effects=True, vmem_limit_bytes=60 * 2**20
            ),
            cost_estimate=pl.CostEstimate(flops=24 * macs, bytes_accessed=10 * 2**20, transcendentals=0),
        )(
            leaf_rhs.reshape(k * nodes, width),
            top_rhs,
            row_map,
            leaf_inverse,
            leaf_below,
            top_inverse,
        )
        return leaf_solution.reshape(k, nodes, width), top_solution

    return on_device


def solution(mesh, nz=8, ny=4):
    placed = (
        P(None, "leaf", "rows"),
        P(),
        P("leaf", "rows", None),
        P("leaf", "rows", None),
        P("leaf", "rows"),
        P(None, "rows", None),
    )
    return jax.shard_map(
        make(nz, ny),
        mesh=mesh,
        in_specs=placed,
        out_specs=(P(None, "leaf", "rows"), P()),
        check_vma=False,
    )
```

```python
import functools

import jax
import jax.numpy as jnp
from jax import lax
from jax.experimental import pallas as pl
from jax.experimental.pallas import tpu as pltpu
from jax.sharding import PartitionSpec as P

F32 = jnp.float32
BF16 = jnp.bfloat16
NN_DIMS = (((1,), (0,)), ((), ()))

NX = 4
G = 4
LANES = 128
H = 2

F_AT = (0, 3, 6, 9)
F_GAP = 3
TOP_AT = ((1, 4, 8, 9, 10, 11, 12), (8, 9, 10, 11, 12, 14, 16))
TAKE_AT = (17, 13)
B_FIRST = 13
B_AT = (0, 3, 6, 9, 12)
B_GAP = 0
LEAVE_AT = 5
STRAIGHT = ((0, 0), (6, 8), (0, 0), (6, 8))
PREP = 3


def split(v):
    hi = v.astype(BF16)
    lo = (v - hi.astype(F32)).astype(BF16)
    return hi, lo


def mm_row(x, w):
    m = x.shape[0]
    hi, lo = split(x)
    o = lax.dot_general(jnp.concatenate([hi, lo], 0), w, NN_DIMS, preferred_element_type=F32)
    return (o[:m, :LANES] + o[:m, LANES:]) + (o[m:, :LANES] + o[m:, LANES:])


def mm_nn(hi, lo, w):
    m = hi.shape[0]
    top = jnp.concatenate([hi, hi], 1)
    low = jnp.concatenate([lo, lo], 1)
    o = lax.dot_general(jnp.concatenate([top, low], 0), w, NN_DIMS, preferred_element_type=F32)
    return o[:m] + o[m:]


def kernel(
    dims,
    rhs_hbm, trhs_hbm, map_hbm, inv_hbm, below_hbm, tinv_hbm,
    leaf_out, top_out,
    rhs_ref, trhs_ref, map_ref, a_f32, b_f32, t_f32, a_hl, b_hl, t_hl, a_t, b_t, t_t, hot_in, hot_out,
    gb, gy, upd, urow, ztop, cbuf, yacc, ybuf, zbuf, xbuf, xbuf2, rvec, hl_in, sol, s_hl,
    pb, pa, r1b, r1a, r2b, r2a,
    in_sem, ssem, rsem, tssem, trsem,
):
    nz, ny = dims
    nodes, k = gb.shape[2], gb.shape[3]
    chunks = nodes // G
    units = H * chunks
    cols = upd.shape[2]
    nt = cols // t_f32.shape[2]
    yrows = urow.shape[1] // ny
    prow = yrows // nz
    kp = prow // 4
    mp = hl_in.shape[0] // 2

    leaf = lax.axis_index("leaf")
    x = lax.axis_index("rows")
    core = lax.rem(leaf, 2)
    y = lax.rem(leaf // 2, ny)
    z = leaf // (2 * ny)
    right, left = lax.rem(x + 1, NX), lax.rem(x + NX - 1, NX)
    opp = lax.rem(x + 2, NX)

    first = y * yrows + z * prow
    t_mine = lax.div(first, 4 * k)

    def leaf_of(zz, yy, cc):
        return (zz * ny + yy) * 2 + cc

    def others(n):
        return sorted(range(1, n), key=lambda d: -min(d, n - d))

    xpeers = [lax.rem(x + d, NX) for d in others(NX)]
    ypeers = [lax.rem(y + d, ny) for d in others(ny)]
    zpeers = [lax.rem(z + d, nz) for d in others(nz)]
    partner = leaf_of(z, y, 1 - core)

    barrier = pltpu.get_barrier_semaphore()
    peers = [{"leaf": leaf_of(p, y, core)} for p in zpeers]
    peers += [{"leaf": leaf_of(z, p, core)} for p in ypeers]
    peers += [{"rows": p} for p in xpeers]
    peers += [{"leaf": partner}]
    for p in peers:
        pl.semaphore_signal(barrier, inc=1, device_id=p, device_id_type=pl.DeviceIdType.MESH)

    def load(which, c):
        src, dst = ((inv_hbm, a_f32), (below_hbm, b_f32))[which]
        return pltpu.make_async_copy(src.at[pl.ds(c * G, G)], dst.at[pl.ds(c * G, G)], in_sem.at[which, c])

    whole = [
        pltpu.make_async_copy(src, dst, in_sem.at[2, i])
        for i, (src, dst) in enumerate(
            ((rhs_hbm, rhs_ref), (map_hbm, map_ref), (tinv_hbm.at[pl.ds(t_mine, 1)], t_f32), (trhs_hbm, trhs_ref))
        )
    ]
    whole[0].start()
    whole[1].start()
    for which in range(2):
        def start_load(c, _, which=which):
            load(which, c).start()
            return 0

        lax.fori_loop(0, chunks, start_load, 0)
    whole[2].start()
    whole[3].start()
    whole[0].wait()

    def fill_own(n, _):
        for h in range(H):
            gb[x, h, n] = rhs_ref[pl.ds(h * k * nodes + n, k, stride=nodes), :]
        return 0

    lax.fori_loop(0, nodes, fill_own, 0)

    def store_both(dst, dst_t, n, v):
        hi, lo = split(v)
        dst[n, 0:LANES, :] = hi
        dst[n, LANES : 2 * LANES, :] = lo
        dst_t[n, :, 0:LANES] = hi.T
        dst_t[n, :, LANES : 2 * LANES] = lo.T

    def prepare(c, _):
        load(0, c).wait()
        for j in range(G):
            store_both(a_hl, a_t, c * G + j, a_f32[c * G + j])
        return 0

    def prepare_below(c):
        load(1, c).wait()
        for j in range(G):
            store_both(b_hl, b_t, c * G + j, b_f32[c * G + j])

    def prepare_in(c, _):
        for j in range(G):
            own = jnp.broadcast_to(map_ref[pl.ds(c * G + j, 1), :], (LANES, LANES)).T
            at = lax.broadcasted_iota(jnp.int32, (LANES, LANES), 1)
            for q in range(cols // LANES):
                hot = jnp.where(own == at + q * LANES, 1.0, 0.0).astype(BF16)
                hot_in[c, j * LANES : (j + 1) * LANES, q * LANES : (q + 1) * LANES] = hot
        return 0

    def prepare_out(u):
        for j in range(G):
            row = map_ref[pl.ds(u * G + j, 1), :]

            def build(s, _, row=row, j=j):
                at = lax.broadcasted_iota(jnp.int32, (256, LANES), 0) + s * 256
                hot = jnp.where(at == row, 1.0, 0.0).astype(BF16)
                hot_out[u, pl.ds(pl.multiple_of(s * 256, 256), 256), j * LANES : (j + 1) * LANES] = hot
                return 0

            lax.fori_loop(0, cols // 256, build, 0)

    whole[1].wait()
    lax.fori_loop(0, PREP, prepare, 0)

    def send(phase, kind, u, src, dst):
        to = opp if kind == 4 else right if kind in (0, 2) else left
        return pltpu.make_async_remote_copy(
            src_ref=src, dst_ref=dst,
            send_sem=ssem.at[phase, kind, u], recv_sem=rsem.at[phase, kind, u],
            device_id={"rows": to}, device_id_type=pl.DeviceIdType.MESH,
        )

    def place(u):
        return lax.div(u, chunks), lax.rem(u, chunks)

    def straight(phase, u):
        low, high = STRAIGHT[phase]
        return (u >= low) & (u < high)

    def gather_direct(phase, u, kind):
        h, c = place(u)
        blk = (gb, gy)[phase].at[x, h, pl.ds(c * G, G)]
        return send(phase, kind, u, blk, blk)

    def gather_forward(phase, u, kind):
        h, c = place(u)
        blk = (gb, gy)[phase].at[left if kind == 2 else right, h, pl.ds(c * G + (kind - 2) * (G // 2), G // 2)]
        return send(phase, kind, u, blk, blk)

    def gather_start(phase, u):
        gather_direct(phase, u, 0).start()
        gather_direct(phase, u, 1).start()

        @pl.when(straight(phase, u))
        def _():
            gather_direct(phase, u, 4).start()

    def gather_pass(phase, u):
        for kind in (0, 1):
            gather_direct(phase, u, kind).wait_recv()

            @pl.when(jnp.logical_not(straight(phase, u)))
            def _(kind=kind):
                gather_forward(phase, u, kind + 2).start()

    def gather_end(phase, u, finish):
        @pl.when(straight(phase, u))
        def _():
            finish(gather_direct(phase, u, 4))

        @pl.when(jnp.logical_not(straight(phase, u)))
        def _():
            finish(gather_forward(phase, u, 2))
            finish(gather_forward(phase, u, 3))

    def arrive(copy):
        copy.wait_recv()

    def leave(copy):
        copy.wait_send()

    pl.semaphore_wait(barrier, len(peers))

    def start_rhs(u, _):
        gather_start(0, u)
        return 0

    lax.fori_loop(0, chunks, start_rhs, 0)

    lax.fori_loop(PREP, chunks, prepare, 0)
    lax.fori_loop(0, chunks, prepare_in, 0)
    whole[2].wait()
    store_both(t_hl, t_t, 0, t_f32[0])
    whole[3].wait()
    for t in range(nt):
        for q in range(4):
            at = (t * 4 + q) * LANES
            ztop[pl.ds(t * 4 * k + q, k, stride=4), :] = trhs_ref[
                pl.ds(pl.multiple_of(core * k, 8), k), at : at + LANES
            ]
    upd[...] = jnp.zeros(upd.shape, F32)
    hl_in[...] = jnp.zeros(hl_in.shape, F32)

    def full_row(buf, h, n):
        return jnp.concatenate([buf[s, h, n] for s in range(NX)], 1)

    def tsend(step, slot, src, dst, to):
        return pltpu.make_async_remote_copy(
            src_ref=src, dst_ref=dst, send_sem=tssem.at[step, slot], recv_sem=trsem.at[step, slot],
            device_id=to, device_id_type=pl.DeviceIdType.MESH,
        )

    def rows_at(start, size):
        return pl.ds(pl.multiple_of(start, 8), size)

    def f0(u):
        gather_pass(0, u)

    def f1(u):
        h, c = place(u)
        gather_end(0, u, arrive)
        for j in range(G):
            n = c * G + j
            gy[x, h, n] = mm_row(full_row(gb, h, n), a_t[n])
        gather_start(1, u)

        @pl.when(u + chunks < units)
        def _():
            gather_start(0, u + chunks)

    def f2(u):
        gather_pass(1, u)

    hand = tsend(0, 0, urow.at[1 - core], cbuf, {"leaf": partner})

    def f3(u):
        h, c = place(u)
        gather_end(1, u, arrive)
        v = [mm_row(full_row(gy, h, c * G + j), b_t[c * G + j]) for j in range(G)]
        hi, lo = split(jnp.concatenate(v, 1))
        lhs = jnp.concatenate([hi, lo], 0)
        width = 512
        for s in range(cols // width):
            o = lax.dot_general(
                lhs, hot_in[c, :, s * width : (s + 1) * width], NN_DIMS, preferred_element_type=F32
            )
            upd[h, :, s * width : (s + 1) * width] += o[:k] + o[k:]

        @pl.when(c == chunks - 1)
        def _():
            for t in range(nt):
                for q in range(4):
                    at = (t * 4 + q) * LANES
                    urow[h, pl.ds(t * 4 * k + q, k, stride=4), :] = upd[h, :, at : at + LANES]

            @pl.when(core != h)
            def _():
                hand.start()

    ysends = [
        tsend(1, d, yacc.at[rows_at(p * yrows, yrows)], ybuf.at[d], {"leaf": leaf_of(z, p, core)})
        for d, p in enumerate(ypeers)
    ]
    ysum = ybuf.at[ny - 1]
    zsends = [
        tsend(2, d, ysum.at[rows_at(p * prow, prow)], zbuf.at[d], {"leaf": leaf_of(p, y, core)})
        for d, p in enumerate(zpeers)
    ]
    xsends = [tsend(3, d, xbuf.at[x], xbuf.at[x], {"rows": p}) for d, p in enumerate(xpeers)]
    xsends2 = [tsend(4, d, xbuf2.at[x], xbuf2.at[x], {"rows": p}) for d, p in enumerate(xpeers)]
    sol_z = sol.at[core, rows_at(first, prow)]
    sol_y = sol.at[core, rows_at(y * yrows, yrows)]
    zback = [tsend(5, d, sol_z, sol_z, {"leaf": leaf_of(p, y, core)}) for d, p in enumerate(zpeers)]
    yback = [tsend(6, d, sol_y, sol_y, {"leaf": leaf_of(z, p, core)}) for d, p in enumerate(ypeers)]
    give = tsend(7, 0, sol.at[core], sol.at[core], {"leaf": partner})

    def begin(sends):
        for s in sends:
            s.start()

    def t0():
        hand.wait_recv()
        yacc[...] = urow[core] + cbuf[...]
        begin(ysends)

    def t1():
        total = yacc[rows_at(y * yrows, yrows), :]
        for d, s in enumerate(ysends):
            s.wait_recv()
            total = total + ybuf[d]
        ysum[...] = total
        begin(zsends)

    def t2():
        total = ysum[rows_at(z * prow, prow), :]
        for d, s in enumerate(zsends):
            s.wait_recv()
            total = total + zbuf[d]
        xbuf[x] = total
        begin(xsends)

    def t3():
        for s in xsends:
            s.wait_recv()
        rvec[...] = ztop[rows_at(first, prow), :] - ((xbuf[0] + xbuf[1]) + (xbuf[2] + xbuf[3]))
        r = jnp.concatenate([rvec[pl.ds(q, kp, stride=4), :] for q in range(4)], 1)
        hi, lo = split(r)
        hl_in[0:kp, :] = hi.astype(F32)
        hl_in[mp : mp + kp, :] = lo.astype(F32)
        o = lax.dot_general(hl_in[...].astype(BF16), t_t[0], NN_DIMS, preferred_element_type=F32)
        f = (o[:mp, :LANES] + o[:mp, LANES:]) + (o[mp:, :LANES] + o[mp:, LANES:])
        hi, lo = split(f)
        fhl = jnp.concatenate([hi.astype(F32), lo.astype(F32)], 0)
        fhl = jnp.concatenate([fhl, fhl], 1).astype(BF16)
        o = lax.dot_general(fhl, t_hl[0], NN_DIMS, preferred_element_type=F32)
        s_part = o[:mp] + o[mp:]
        for q in range(4):
            rvec[pl.ds(q, kp, stride=4), :] = s_part[0:kp, q * LANES : (q + 1) * LANES]
        xbuf2[x] = rvec[...]
        begin(xsends2)

    def t4():
        for s in xsends2:
            s.wait_recv()
        sol[core, rows_at(first, prow), :] = (xbuf2[0] + xbuf2[1]) + (xbuf2[2] + xbuf2[3])
        begin(zback)

    def t5():
        for s in zback:
            s.wait_recv()
        begin(yback)

    def t6():
        for s in yback:
            s.wait_recv()
        give.start()
        unpack(core)

    def take():
        tsend(7, 0, sol.at[1 - core], sol.at[1 - core], {"leaf": partner}).wait_recv()
        unpack(1 - core)

    def unpack(h):
        for t in range(nt):
            for q in range(4):
                v = sol[h, pl.ds(t * 4 * k + q, k, stride=4), :]
                at = (t * 4 + q) * LANES
                top_out[pl.ds(pl.multiple_of(h * k, 8), k), at : at + LANES] = v
                hi, lo = split(v)
                s_hl[h, 0:k, at : at + LANES] = hi
                s_hl[h, k : 2 * k, at : at + LANES] = lo

    def toward_opp(phase, u, kind):
        h, c = place(u)
        ns = pl.ds(c * G + kind * (G // 2), G // 2)
        buf, r1 = ((pb, r1b), (pa, r1a))[phase - 2]
        return send(phase, kind, u, buf.at[opp, h, ns], r1.at[h, ns])

    def toward_next(phase, u, kind):
        h, c = place(u)
        ns = pl.ds(c * G, G)
        buf, r2 = ((pb, r2b), (pa, r2a))[phase - 2]
        return send(phase, kind, u, buf.at[(right, left, opp)[kind - 2], h, ns], r2.at[kind - 2, h, ns])

    def put(buf, h, n, v):
        for s in range(NX):
            buf[s, h, n] = v[:, s * LANES : (s + 1) * LANES]

    def reduce_start(phase, u):
        @pl.when(straight(phase, u))
        def _():
            for kind in (2, 3, 4):
                toward_next(phase, u, kind).start()

        @pl.when(jnp.logical_not(straight(phase, u)))
        def _():
            toward_opp(phase, u, 0).start()
            toward_opp(phase, u, 1).start()

    def reduce_pass(phase, u):
        @pl.when(jnp.logical_not(straight(phase, u)))
        def _():
            h, c = place(u)
            buf, r1 = ((pb, r1b), (pa, r1a))[phase - 2]
            for kind, to in ((0, right), (1, left)):
                ns = pl.ds(c * G + kind * (G // 2), G // 2)
                toward_opp(phase, u, kind).wait_recv()
                buf[to, h, ns] += r1[h, ns]
                toward_next(phase, u, kind + 2).start()

    def reduce_end(phase, u):
        h, c = place(u)
        buf, r2 = ((pb, r2b), (pa, r2a))[phase - 2]
        ns = pl.ds(c * G, G)

        @pl.when(straight(phase, u))
        def _():
            toward_next(phase, u, 4).wait_recv()
            buf[x, h, ns] += r2[2, h, ns]

        toward_next(phase, u, 2).wait_recv()
        toward_next(phase, u, 3).wait_recv()
        return buf[x, h, ns] + (r2[0, h, ns] + r2[1, h, ns])

    def reduce_leave(phase, u):
        toward_next(phase, u, 2).wait_send()
        toward_next(phase, u, 3).wait_send()

        @pl.when(straight(phase, u))
        def _():
            toward_next(phase, u, 4).wait_send()

        @pl.when(jnp.logical_not(straight(phase, u)))
        def _():
            toward_opp(phase, u, 0).wait_send()
            toward_opp(phase, u, 1).wait_send()

    def b0(u):
        h, c = place(u)
        picked = lax.dot_general(s_hl[h], hot_out[c], NN_DIMS, preferred_element_type=F32).astype(BF16)
        for j in range(G):
            at = slice(j * LANES, (j + 1) * LANES)
            put(pb, h, c * G + j, mm_nn(picked[:k, at], picked[k:, at], b_hl[c * G + j]))
        reduce_start(2, u)

    def b1(u):
        reduce_pass(2, u)

    def b2(u):
        h, c = place(u)
        back = reduce_end(2, u)
        for j in range(G):
            n = c * G + j
            hi, lo = split(gy[x, h, n] - back[j])
            put(pa, h, n, mm_nn(hi, lo, a_hl[n]))
        reduce_start(3, u)

    def b3(u):
        reduce_pass(3, u)

    def b4(u):
        h, c = place(u)
        reduce_leave(2, u)
        done = reduce_end(3, u)
        for j in range(G):
            leaf_out[pl.ds(h * k * nodes + c * G + j, k, stride=nodes), :] = done[j]

    def leave_forward(u):
        for phase in (0, 1):
            gather_direct(phase, u, 0).wait_send()
            gather_direct(phase, u, 1).wait_send()
            gather_end(phase, u, leave)

    base = F_AT[3] + chunks - 1
    b_base = base + B_FIRST

    tops = (t0, t1, t2, t3, t4, t5, t6)
    forwards = ((0, f0), (2, f2), (1, f1), (3, f3))
    backwards = ((1, b1), (3, b3), (4, b4), (2, b2), (0, b0))

    def run(low, high):
        def holds(at, gap):
            return at < high and at + units + gap > low

        def step(i, _):
            def unit_at(at, gap, body):
                v = i - at
                second = v >= chunks + gap

                @pl.when(((v >= 0) & (v < chunks)) | (second & (v < units + gap)))
                def _():
                    body(jnp.where(second, v - gap, v))

            def when_at(ats, body):
                for c, at in enumerate(ats):
                    if low <= base + at < high:
                        pl.when((core == c) & (i == base + at))(body)

            for j, body in enumerate(tops):
                when_at((TOP_AT[0][j], TOP_AT[1][j]), body)
            when_at(TAKE_AT, take)
            for j, body in forwards:
                if holds(F_AT[j], F_GAP):
                    unit_at(F_AT[j], F_GAP, body)
                if j == 0 and low == 0:
                    pl.when(i < chunks)(lambda: prepare_below(i))
            if holds(base + 1, 0):
                pl.when((i > base) & (i <= base + chunks))(lambda: prepare_out(i - base - 1))
            if holds(base + LEAVE_AT, 0):
                unit_at(base + LEAVE_AT, 0, leave_forward)
            for j, body in backwards:
                if holds(b_base + B_AT[j], B_GAP):
                    unit_at(b_base + B_AT[j], B_GAP, body)
            return 0

        lax.fori_loop(low, high, step, 0)

    run(0, base + 1)
    run(base + 1, b_base)
    run(b_base, b_base + B_AT[4] + units + B_GAP)

    def drain(u, _):
        reduce_leave(3, u)
        return 0

    lax.fori_loop(0, units, drain, 0)
    for s in [hand, give] + ysends + zsends + xsends + xsends2 + zback + yback:
        s.wait_send()


def make(nz, ny):
    def on_device(leaf_rhs, top_rhs, leaf_inverse, leaf_below, row_map, top_inverse):
        k, nodes, width = leaf_rhs.shape
        s = top_inverse.shape[2]
        full = leaf_inverse.shape[2]
        cols = top_rhs.shape[1]
        chunks = nodes // G
        rows = cols * k // LANES
        half = rows // H
        kh = k // H
        units = H * chunks
        yrows = half // ny
        prow = yrows // nz
        mp = max(8, prow // 4)
        vmem = pl.BlockSpec(memory_space=pltpu.VMEM)
        hbm = pl.BlockSpec(memory_space=pltpu.HBM)
        blocks = (NX, H, nodes, kh, LANES)
        scratch = [
            pltpu.VMEM((k * nodes, width), F32),
            pltpu.VMEM((k, cols), F32),
            pltpu.VMEM((nodes, width), jnp.int32),
            pltpu.VMEM(leaf_inverse.shape, F32),
            pltpu.VMEM(leaf_below.shape, F32),
            pltpu.VMEM((1,) + top_inverse.shape[1:], F32),
            pltpu.VMEM((nodes, 2 * LANES, full), BF16),
            pltpu.VMEM((nodes, 2 * LANES, full), BF16),
            pltpu.VMEM((1, 2 * LANES, s), BF16),
            pltpu.VMEM((nodes, full, 2 * LANES), BF16),
            pltpu.VMEM((nodes, full, 2 * LANES), BF16),
            pltpu.VMEM((1, s, 2 * LANES), BF16),
            pltpu.VMEM((chunks, G * LANES, cols), BF16),
            pltpu.VMEM((chunks, cols, G * LANES), BF16),
            pltpu.VMEM(blocks, F32),
            pltpu.VMEM(blocks, F32),
            pltpu.VMEM((H, kh, cols), F32),
            pltpu.VMEM((H, half, LANES), F32),
            pltpu.VMEM((half, LANES), F32),
            pltpu.VMEM((half, LANES), F32),
            pltpu.VMEM((half, LANES), F32),
            pltpu.VMEM((ny, yrows, LANES), F32),
            pltpu.VMEM((nz, prow, LANES), F32),
            pltpu.VMEM((NX, prow, LANES), F32),
            pltpu.VMEM((NX, prow, LANES), F32),
            pltpu.VMEM((prow, LANES), F32),
            pltpu.VMEM((2 * mp, s), F32),
            pltpu.VMEM((H, half, LANES), F32),
            pltpu.VMEM((H, 2 * kh, cols), BF16),
            pltpu.VMEM(blocks, F32),
            pltpu.VMEM(blocks, F32),
            pltpu.VMEM(blocks[1:], F32),
            pltpu.VMEM(blocks[1:], F32),
            pltpu.VMEM((3,) + blocks[1:], F32),
            pltpu.VMEM((3,) + blocks[1:], F32),
            pltpu.SemaphoreType.DMA((3, max(chunks, 4))),
            pltpu.SemaphoreType.DMA((4, 5, units)),
            pltpu.SemaphoreType.DMA((4, 5, units)),
            pltpu.SemaphoreType.DMA((8, 8)),
            pltpu.SemaphoreType.DMA((8, 8)),
        ]
        macs = nodes * width * full * k
        leaf_solution, top_solution = pl.pallas_call(
            functools.partial(kernel, (nz, ny)),
            out_shape=(
                jax.ShapeDtypeStruct((k * nodes, width), F32),
                jax.ShapeDtypeStruct((k, cols), F32),
            ),
            in_specs=[hbm] * 6,
            out_specs=(vmem, vmem),
            scratch_shapes=scratch,
            compiler_params=pltpu.CompilerParams(
                collective_id=0, has_side_effects=True, vmem_limit_bytes=60 * 2**20
            ),
            cost_estimate=pl.CostEstimate(flops=24 * macs, bytes_accessed=10 * 2**20, transcendentals=0),
        )(
            leaf_rhs.reshape(k * nodes, width),
            top_rhs,
            row_map,
            leaf_inverse,
            leaf_below,
            top_inverse,
        )
        return leaf_solution.reshape(k, nodes, width), top_solution

    return on_device


def solution(mesh, nz=8, ny=4):
    placed = (
        P(None, "leaf", "rows"),
        P(),
        P("leaf", "rows", None),
        P("leaf", "rows", None),
        P("leaf", "rows"),
        P(None, "rows", None),
    )
    return jax.shard_map(
        make(nz, ny),
        mesh=mesh,
        in_specs=placed,
        out_specs=(P(None, "leaf", "rows"), P()),
        check_vma=False,
    )
```
